32 devices in a mesh: sec: 4 (over y, x), lat: 8 (over z, core).
Axes of the slice: x: 2, y: 2, z: 4, core: 2. Of those that a mesh axis runs over, the one named last changes fastest.
Arguments:
- states: float32 [4, 3, 448, 4096], P('sec', None, 'lat'), may hold values from -40 to 40
- depth_field: float32 [448, 4096], P('lat'), may hold values from 0.07 to 1
- land_mask: int32 [448, 4096], P('lat'), may hold values 0 or 1
- tide_cos: float32 [448, 4096], P('lat'), may hold values from -8 to 8
- tide_sin: float32 [448, 4096], P('lat'), may hold values from -8 to 8
Outputs:
- new_states: float32 [4, 3, 448, 4096], P('sec', None, 'lat')
- mismatch: float32 [4, 3, 448, 4096], P('sec', None, 'lat')
- step_length: float32 [], replicated
The draws below stay inside these ranges and needn't reach their ends.
All inputs are finite; a program needn't handle non-finite values. No bound on the sum of `land_mask` on one device may be relied on, other than what follows from the above.
Results may differ from the reference program's by a relative error of at most 0.00002.
Values sent between devices are 32-bit elements; how exact they have to be, the bound alone decides.
A program may use at most 64 MiB of HBM per device.

```python
import math
import jax
import jax.numpy as jnp

LON = 4096
STEPS = 4
SECTIONS = 4
LATS = 448


def draw_states(key, part):
    key_base, key_rough = jax.random.split(key, 2)
    shape_all = (SECTIONS, 3, LATS, LON)
    base_values = jax.random.normal(key_base, shape_all, jnp.float32)
    rough_factor = jnp.exp(jax.random.uniform(key_rough, shape_all, jnp.float32, -0.7, 0.7))
    lat_ramp = 1.0 + 2.0 * jnp.arange(LATS, dtype=jnp.float32) / max(LATS - 1, 1)
    sec_ramp = 1.0 + jnp.arange(SECTIONS, dtype=jnp.float32) / max(SECTIONS - 1, 1)
    return 0.4 * base_values * rough_factor * lat_ramp[None, None, :, None] * sec_ramp[:, None, None, None]


def block_levels(key, row_low, row_high, col_low, col_high):
    key_row, key_col = jax.random.split(key, 2)
    row_levels = jax.random.uniform(key_row, (LATS // 8 + 1,), jnp.float32, row_low, row_high)
    col_levels = jax.random.uniform(key_col, (8,), jnp.float32, col_low, col_high)
    row_block = jnp.arange(LATS, dtype=jnp.int32) // 8
    col_block = jnp.arange(LON, dtype=jnp.int32) * 8 // LON
    return row_levels[row_block][:, None] + col_levels[col_block][None, :]


def draw_depth_field(key, part):
    key_level, key_cell = jax.random.split(jax.random.fold_in(key, 11), 2)
    levels = block_levels(key_level, -1.2, 0.0, -0.6, 0.0)
    cell_levels = jax.random.uniform(key_cell, (LATS, LON), jnp.float32, -0.35, 0.0)
    return jnp.exp(levels + cell_levels)


def tide_draw(key, constant):
    key_level, key_value = jax.random.split(jax.random.fold_in(key, constant), 2)
    levels = block_levels(key_level, -0.8, 0.8, -0.4, 0.4)
    values = jnp.clip(jax.random.normal(key_value, (LATS, LON), jnp.float32), -4.0, 4.0)
    return jnp.clip(values * jnp.exp(levels), -8.0, 8.0)


def draw_tide_cos(key, part):
    return tide_draw(key, 23)


def draw_tide_sin(key, part):
    return tide_draw(key, 37)


def plant(entries, stream_key, low, top_value):
    longest = entries.shape.index(max(entries.shape))
    spots = []
    for shift in (0, 1):
        where = [jax.random.randint(jax.random.fold_in(stream_key, axis), (), 0, length) for axis, length in enumerate(entries.shape)]
        where[longest] = (where[longest] + shift) % entries.shape[longest]
        spots.append(tuple(where))
    return entries.at[spots[0]].set(low).at[spots[1]].set(top_value)


def setup_inputs(seed: int = 0) -> dict:
    key_of = jax.random.split(jax.random.key(seed), 6)
    return {
        "states": draw_states(jax.random.fold_in(key_of[5], 71), 0),
        "depth_field": draw_depth_field(jax.random.fold_in(key_of[5], 71), 0),
        "land_mask": plant((jax.random.randint(key_of[2], (LATS, LON), 0, 10) < 7).astype(jnp.int32), jax.random.fold_in(key_of[2], 1), 0, 1),
        "tide_cos": draw_tide_cos(jax.random.fold_in(key_of[5], 71), 0),
        "tide_sin": draw_tide_sin(jax.random.fold_in(key_of[5], 71), 0),
    }


DRAG_RATE = 0.9
CORIOLIS_MAX = 0.3
PUSH_RATE = 1.0
FLOW_RATE = 1.0
EPSILON = 1e-6
TWO_PI = 2.0 * math.pi


def along_lon(source):
    return 0.5 * (jnp.roll(source, -1, axis=-1) - jnp.roll(source, 1, axis=-1))


def along_lat(source):
    widths = [(0, 0)] * (source.ndim - 2) + [(1, 1), (0, 0)]
    padded = jnp.pad(source, widths)
    return 0.5 * (padded[..., 2:, :] - padded[..., :-2, :])


def forward_step(height, east_flow, north_flow, wet_field, sea_field, coriolis, forcing):
    raised = height + forcing
    east_new = sea_field * (DRAG_RATE * east_flow + coriolis * north_flow - PUSH_RATE * along_lon(raised))
    north_new = sea_field * (DRAG_RATE * north_flow - coriolis * east_flow - PUSH_RATE * along_lat(raised))
    height_new = height - FLOW_RATE * along_lon(wet_field * east_new) - FLOW_RATE * along_lat(wet_field * north_new)
    return height_new, east_new, north_new


def adjoint_step(height_cot, east_cot, north_cot, wet_field, sea_field, coriolis):
    east_mid = sea_field * (east_cot + FLOW_RATE * wet_field * along_lon(height_cot))
    north_mid = sea_field * (north_cot + FLOW_RATE * wet_field * along_lat(height_cot))
    height_new = height_cot + PUSH_RATE * along_lon(east_mid) + PUSH_RATE * along_lat(north_mid)
    east_new = DRAG_RATE * east_mid - coriolis * north_mid
    north_new = coriolis * east_mid + DRAG_RATE * north_mid
    return height_new, east_new, north_new


def reference(states, depth_field, land_mask, tide_cos, tide_sin):
    sea_field = land_mask.astype(jnp.float32)
    wet_field = depth_field * sea_field
    row_values = jnp.arange(LATS, dtype=jnp.int32).astype(jnp.float32)
    coriolis = (CORIOLIS_MAX * jnp.sin(jnp.pi * (row_values + 0.5) / LATS - 0.5 * jnp.pi))[:, None]

    def integrate(fields, forced):
        height, east_flow, north_flow = fields[:, 0], fields[:, 1], fields[:, 2]
        for segment_index in range(STEPS):
            if forced:
                phase_angle = TWO_PI * (jnp.arange(SECTIONS, dtype=jnp.int32) * STEPS + segment_index).astype(jnp.float32) / (SECTIONS * STEPS)
                forcing = jnp.cos(phase_angle)[:, None, None] * tide_cos + jnp.sin(phase_angle)[:, None, None] * tide_sin
            else:
                forcing = jnp.zeros((), jnp.float32)
            height, east_flow, north_flow = forward_step(height, east_flow, north_flow, wet_field, sea_field, coriolis, forcing)
        return jnp.stack([height, east_flow, north_flow], axis=1)

    ending = integrate(states, True)
    mismatch = ending - jnp.roll(states, -1, axis=0)
    height, east_flow, north_flow = mismatch[:, 0], mismatch[:, 1], mismatch[:, 2]
    for segment_index in range(STEPS):
        height, east_flow, north_flow = adjoint_step(height, east_flow, north_flow, wet_field, sea_field, coriolis)
    adjoint = jnp.stack([height, east_flow, north_flow], axis=1)
    gradient = adjoint - jnp.roll(mismatch, 1, axis=0)
    image = integrate(gradient, False) - jnp.roll(gradient, -1, axis=0)
    total_count = SECTIONS * 3 * LATS * LON
    grad_mean = jnp.sum(gradient * gradient) / total_count
    image_mean = jnp.sum(image * image) / total_count
    step_length = grad_mean / (image_mean + EPSILON)
    new_states = states - step_length * gradient
    return new_states, mismatch, step_length
```

```python
import functools
import math

import jax
import jax.numpy as jnp
import numpy as np
from jax import lax
from jax.experimental import pallas as pl
from jax.experimental.pallas import tpu as pltpu
from jax.sharding import PartitionSpec as P

STEPS = 4
DRAG_RATE = 0.9
CORIOLIS_MAX = 0.3
EPSILON = 1e-06
TWO_PI = 2.0 * math.pi
HALO = 24
SIDE = 128
MESH = pl.DeviceIdType.MESH


def kernel(
    sections, bands, count,
    states, depth, mask, tide_one, tide_two, rows_in, trig,
    new_states, mismatch, step_out,
    wide, mask_win, st, start, mis, grad, full,
    high, east, north, raised, flux, acc, part, total,
    load_sem, s1, r1, halo_s, halo_r, st_s, st_r, s2, r2, s3, r3, own_sem, ps, pr, ts, tr,
):
    me = lax.axis_index("sec")
    band = lax.axis_index("lat")
    rows, lon = states.shape[1], states.shape[2]
    share = lon // sections
    win = share + 2 * SIDE
    tall = rows + 2 * HALO
    strips = tall // 8
    top, low = HALO, HALO + rows

    def peer(i):
        return lax.rem(me + i, sections)

    loads = []

    def load(src, dst):
        c = pltpu.make_async_copy(src, dst, load_sem.at[len(loads)])
        c.start()
        loads.append(c)

    load(states.at[:, :, :], wide.at[:, :, pl.ds(SIDE, lon)])
    load(states.at[:, :, pl.ds(lon - SIDE, SIDE)], wide.at[:, :, pl.ds(0, SIDE)])
    load(states.at[:, :, pl.ds(0, SIDE)], wide.at[:, :, pl.ds(SIDE + lon, SIDE)])
    mid = pl.multiple_of(me * share, 128)
    left = pl.multiple_of(lax.rem(me * share + lon - SIDE, lon), 128)
    right = pl.multiple_of(lax.rem(me * share + share, lon), 128)
    for src, dst in (
        (depth, st.at[0, pl.ds(top, rows)]),
        (mask, mask_win),
        (tide_one, st.at[2, pl.ds(top, rows)]),
        (tide_two, st.at[3, pl.ds(top, rows)]),
    ):
        load(src.at[:, pl.ds(mid, share)], dst.at[:, pl.ds(SIDE, share)])
        load(src.at[:, pl.ds(left, SIDE)], dst.at[:, pl.ds(0, SIDE)])
        load(src.at[:, pl.ds(right, SIDE)], dst.at[:, pl.ds(SIDE + share, SIDE)])

    barrier = pltpu.get_barrier_semaphore()
    for i in range(1, sections):
        pl.semaphore_signal(barrier, inc=1, device_id={"sec": peer(i)}, device_id_type=MESH)
    for i in range(1, bands):
        pl.semaphore_signal(
            barrier, inc=1, device_id={"lat": lax.rem(band + i, bands)}, device_id_type=MESH
        )
    pl.semaphore_wait(barrier, sections + bands - 2)

    for c in loads[:3]:
        c.wait()

    def piece(j, slot):
        return pltpu.make_async_remote_copy(
            src_ref=wide.at[:, :, pl.ds(pl.multiple_of(j * share, 128), win)],
            dst_ref=start.at[me, :, pl.ds(top, rows), :],
            send_sem=s1.at[j],
            recv_sem=r1.at[slot],
            device_id={"sec": j},
            device_id_type=MESH,
        )

    for i in range(1, sections):
        piece(peer(i), me).start()
    own = pltpu.make_async_copy(
        wide.at[:, :, pl.ds(pl.multiple_of(me * share, 128), win)],
        start.at[me, :, pl.ds(top, rows), :],
        own_sem.at[0],
    )
    own.start()

    up_ok, down_ok = band > 0, band < bands - 1

    def to_above(s):
        return pltpu.make_async_remote_copy(
            src_ref=start.at[s, :, pl.ds(top, HALO), :],
            dst_ref=start.at[s, :, pl.ds(low, HALO), :],
            send_sem=halo_s.at[0, s], recv_sem=halo_r.at[0, s],
            device_id={"lat": band - 1}, device_id_type=MESH,
        )

    def to_below(s):
        return pltpu.make_async_remote_copy(
            src_ref=start.at[s, :, pl.ds(low - HALO, HALO), :],
            dst_ref=start.at[s, :, pl.ds(0, HALO), :],
            send_sem=halo_s.at[1, s], recv_sem=halo_r.at[1, s],
            device_id={"lat": band + 1}, device_id_type=MESH,
        )

    def st_above():
        return pltpu.make_async_remote_copy(
            src_ref=st.at[:, pl.ds(top, HALO), :], dst_ref=st.at[:, pl.ds(low, HALO), :],
            send_sem=st_s.at[0], recv_sem=st_r.at[0],
            device_id={"lat": band - 1}, device_id_type=MESH,
        )

    def st_below():
        return pltpu.make_async_remote_copy(
            src_ref=st.at[:, pl.ds(low - HALO, HALO), :], dst_ref=st.at[:, pl.ds(0, HALO), :],
            send_sem=st_s.at[1], recv_sem=st_r.at[1],
            device_id={"lat": band + 1}, device_id_type=MESH,
        )

    def send_halo(s):
        @pl.when(up_ok)
        def _():
            to_above(s).start()

        @pl.when(down_ok)
        def _():
            to_below(s).start()

    def recv_halo(s):
        @pl.when(down_ok)
        def _():
            to_above(s).wait_recv()

        @pl.when(up_ok)
        def _():
            to_below(s).wait_recv()

    own.wait()
    send_halo(me)

    for c in loads[3:]:
        c.wait()

    def prepare(r, _):
        at = pl.ds(pl.multiple_of(top + 8 * r, 8), 8)
        sea = mask_win[pl.ds(pl.multiple_of(8 * r, 8), 8), :].astype(jnp.float32)
        st[1, at, :] = sea
        st[0, at, :] = st[0, at, :] * sea
        return 0

    lax.fori_loop(0, rows // 8, prepare, 0)

    @pl.when(up_ok)
    def _():
        st_above().start()

    @pl.when(down_ok)
    def _():
        st_below().start()

    def blank(first):
        def body(r, _):
            at = pl.ds(pl.multiple_of(first + 8 * r, 8), 8)
            zero = jnp.zeros((8, win), jnp.float32)
            for a in range(4):
                st[a, at, :] = zero
            for s in range(sections):
                for a in range(3):
                    start[s, a, at, :] = zero
            return 0

        lax.fori_loop(0, HALO // 8, body, 0)

    @pl.when(band == 0)
    def _():
        blank(0)

    @pl.when(band == bands - 1)
    def _():
        blank(low)

    zero = jnp.zeros((8, win), jnp.float32)
    for buf in (raised, flux):
        buf[pl.ds(0, 8), :] = zero
        buf[pl.ds(8 + tall, 8), :] = zero
    acc[...] = jnp.zeros_like(acc)

    @pl.when(down_ok)
    def _():
        st_above().wait_recv()

    @pl.when(up_ok)
    def _():
        st_below().wait_recv()

    def lon_diff(x):
        return pltpu.roll(x, win - 1, 1) - pltpu.roll(x, 1, 1)

    row = lax.broadcasted_iota(jnp.int32, (8, win), 0)

    def lat_diff(ref, at):
        before, here, after = (ref[pl.ds(pl.multiple_of(at + 8 * i, 8), 8), :] for i in range(3))
        down = pltpu.roll(jnp.where(row == 7, before, here), 1, 0)
        up = pltpu.roll(jnp.where(row == 0, after, here), 7, 0)
        return up - down

    def run(kind, source, s, lo, hi, finish):
        def push(h, at, step):
            if kind != "forced":
                return 0.5 * h
            base = 2 * (s * STEPS + step)
            push_now = trig[base] * st[2, at, :] + trig[base + 1] * st[3, at, :]
            return 0.5 * (h + push_now)

        def begin(r, _):
            r0 = pl.multiple_of(8 * r, 8)
            at = pl.ds(r0, 8)
            h = source[s, 0, at, :]
            high[at, :] = h
            east[at, :] = source[s, 1, at, :]
            north[at, :] = source[s, 2, at, :]
            raised[pl.ds(pl.multiple_of(r0 + 8, 8), 8), :] = push(h, at, 0)
            return 0

        lax.fori_loop(lo, hi, begin, 0)
        if lo > 0:
            raised[pl.ds(8 * lo, 8), :] = zero
            raised[pl.ds(8 * hi + 8, 8), :] = zero
            flux[pl.ds(8 * lo, 8), :] = zero
            flux[pl.ds(8 * hi + 8, 8), :] = zero
        for step in range(STEPS):
            def first(r, _):
                r0 = pl.multiple_of(8 * r, 8)
                at = pl.ds(r0, 8)
                wet, sea = st[0, at, :], st[1, at, :]
                cor = rows_in[0, at, :][:, :1]
                x = raised[pl.ds(pl.multiple_of(r0 + 8, 8), 8), :]
                dx, dy = lon_diff(x), lat_diff(raised, r0)
                u, v, h = east[at, :], north[at, :], high[at, :]
                if kind == "back":
                    e = sea * (u + wet * dx)
                    f = sea * (v + wet * dy)
                    east[at, :] = DRAG_RATE * e - cor * f
                    north[at, :] = cor * e + DRAG_RATE * f
                    flux[pl.ds(pl.multiple_of(r0 + 8, 8), 8), :] = 0.5 * f
                    high[at, :] = h + lon_diff(0.5 * e)
                else:
                    e = sea * (DRAG_RATE * u + cor * v - dx)
                    f = sea * (DRAG_RATE * v - cor * u - dy)
                    east[at, :] = e
                    north[at, :] = f
                    half = 0.5 * wet
                    flux[pl.ds(pl.multiple_of(r0 + 8, 8), 8), :] = half * f
                    high[at, :] = h - lon_diff(half * e)
                return 0

            lax.fori_loop(lo, hi, first, 0)

            def second(r, _):
                r0 = pl.multiple_of(8 * r, 8)
                at = pl.ds(r0, 8)
                inside = rows_in[1, at, :][:, :1]
                dy = lat_diff(flux, r0)
                h = high[at, :]
                h = (h + dy if kind == "back" else h - dy) * inside
                if step == STEPS - 1:
                    finish(at, h, east[at, :], north[at, :])
                else:
                    high[at, :] = h
                    raised[pl.ds(pl.multiple_of(r0 + 8, 8), 8), :] = push(h, at, step + 1)
                return 0

            lax.fori_loop(lo, hi, second, 0)

    def squares(x):
        x = x[:, SIDE:SIDE + share]
        x = x * x
        return sum(x[:, i * 128:(i + 1) * 128] for i in range(share // 128))

    recv_halo(me)

    def keep(at, h, u, v):
        for a, x in enumerate((h, u, v)):
            mis[me, a, at, :] = x

    run("forced", start, me, 0, strips, keep)

    def arrive(i, _):
        s = peer(i)
        piece(s, s).wait_recv()
        send_halo(s)
        return 0

    lax.fori_loop(1, sections, arrive, 0)

    def arrive_halo(i, _):
        recv_halo(peer(i))
        return 0

    lax.fori_loop(1, sections, arrive_halo, 0)

    def mine(r, _):
        at = pl.ds(pl.multiple_of(8 * r, 8), 8)
        for a in range(3):
            mis[me, a, at, :] = mis[me, a, at, :] - start[peer(1), a, at, :]
        return 0

    lax.fori_loop(0, strips, mine, 0)
    columns = pl.ds(pl.multiple_of(me * share, 128), share)
    own_mis = pltpu.make_async_copy(
        mis.at[me, :, pl.ds(top, rows), pl.ds(SIDE, share)],
        mismatch.at[:, :, columns],
        own_sem.at[1],
    )
    own_mis.start()

    def give(source, target, send, recv, s, at_columns, slot):
        return pltpu.make_async_remote_copy(
            src_ref=source.at[s, :, pl.ds(top, rows), pl.ds(SIDE, share)],
            dst_ref=target.at[:, :, at_columns],
            send_sem=send.at[s], recv_sem=recv.at[slot],
            device_id={"sec": s}, device_id_type=MESH,
        )

    def forced(i, _):
        s = peer(i)
        after = peer(i + 1)

        def done(at, h, u, v):
            for a, x in enumerate((h, u, v)):
                mis[s, a, at, :] = x - start[after, a, at, :]

        run("forced", start, s, 0, strips, done)
        give(mis, mismatch, s2, r2, s, columns, me).start()
        return 0

    lax.fori_loop(1, sections, forced, 0)

    def back(i, _):
        s = peer(i)
        before = peer(i + sections - 1)

        def done(at, h, u, v):
            for a, x in enumerate((h, u, v)):
                grad[s, a, at, :] = x - mis[before, a, at, :]

        run("back", mis, s, 1, strips - 1, done)

        @pl.when(i < sections)
        def _():
            give(grad, full, s3, r3, s, columns, me).start()

        return 0

    lax.fori_loop(1, sections + 1, back, 0)
    own_grad = pltpu.make_async_copy(
        grad.at[me, :, pl.ds(top, rows), pl.ds(SIDE, share)],
        full.at[:, :, columns],
        own_sem.at[2],
    )
    own_grad.start()

    def image(i, _):
        s = peer(i)
        after = peer(i + 1)

        def done(at, h, u, v):
            for a, x in enumerate((h, u, v)):
                g = grad[after, a, at, :]
                acc[1] += squares(x - g)
                acc[0] += squares(g)

        def outer(at, h, u, v):
            done(at, h, u, v)

        run_image(s, outer)
        return 0

    def run_image(s, finish):
        run("free", grad, s, 2, strips - 2, lambda at, h, u, v: store(at, h, u, v))

        def gather(r, _):
            at = pl.ds(pl.multiple_of(8 * r, 8), 8)
            finish(at, high[at, :], east[at, :], north[at, :])
            return 0

        lax.fori_loop(HALO // 8, (HALO + rows) // 8, gather, 0)

    def store(at, h, u, v):
        high[at, :] = h

    lax.fori_loop(0, sections, image, 0)

    part[me] = acc[...]

    def share_part(j, slot):
        return pltpu.make_async_remote_copy(
            src_ref=acc, dst_ref=part.at[slot], send_sem=ps.at[j], recv_sem=pr.at[slot],
            device_id={"sec": j}, device_id_type=MESH,
        )

    for i in range(1, sections):
        share_part(peer(i), me).start()
    for i in range(1, sections):
        share_part(peer(i), peer(i)).wait_recv()
    for i in range(1, sections):
        share_part(peer(i), me).wait_send()
    summed = part[0]
    for s in range(1, sections):
        summed = summed + part[s]
    acc[...] = summed
    total[band] = summed

    def share_total(j, slot):
        return pltpu.make_async_remote_copy(
            src_ref=acc, dst_ref=total.at[slot], send_sem=ts.at[j], recv_sem=tr.at[slot],
            device_id={"lat": j}, device_id_type=MESH,
        )

    for i in range(1, bands):
        share_total(lax.rem(band + i, bands), band).start()
    for i in range(1, bands):
        j = lax.rem(band + i, bands)
        share_total(j, j).wait_recv()
    summed = total[0]
    for s in range(1, bands):
        summed = summed + total[s]
    sums = jnp.sum(jnp.sum(summed, axis=2, keepdims=True), axis=1, keepdims=True)
    step = sums[0] / count / (sums[1] / count + EPSILON)
    step_out[...] = jnp.broadcast_to(step, (8, 128))

    own_grad.wait()

    def grads(i, _):
        s = peer(i)
        give(grad, full, s3, r3, s, columns, s).wait_recv()
        return 0

    lax.fori_loop(1, sections, grads, 0)

    def update(r, _):
        at = pl.ds(pl.multiple_of(8 * r, 8), 8)
        for a in range(3):
            new_states[a, at, :] = wide[a, at, SIDE:SIDE + lon] - step * full[a, at, :]
        return 0

    lax.fori_loop(0, rows // 8, update, 0)

    own_mis.wait()

    def drain(i, _):
        s = peer(i)
        piece(s, me).wait_send()
        give(mis, mismatch, s2, r2, s, columns, s).wait()
        give(grad, full, s3, r3, s, columns, me).wait_send()
        return 0

    lax.fori_loop(1, sections, drain, 0)

    def drain_halo(i, _):
        s = peer(i)

        @pl.when(up_ok)
        def _():
            to_above(s).wait_send()

        @pl.when(down_ok)
        def _():
            to_below(s).wait_send()

        return 0

    lax.fori_loop(0, sections, drain_halo, 0)

    @pl.when(up_ok)
    def _():
        st_above().wait_send()

    @pl.when(down_ok)
    def _():
        st_below().wait_send()

    for i in range(1, bands):
        share_total(lax.rem(band + i, bands), band).wait_send()


def shards(states, depth_field, land_mask, tide_cos, tide_sin):
    fields = states[0]
    rows, lon = fields.shape[1:]
    sections, bands = lax.axis_size("sec"), lax.axis_size("lat")
    band = lax.axis_index("lat")
    share = lon // sections
    win = share + 2 * SIDE
    tall = rows + 2 * HALO
    lat_total = rows * bands
    ids = band * rows - HALO + jnp.arange(tall, dtype=jnp.int32)
    inside = ((ids >= 0) & (ids < lat_total)).astype(jnp.float32)
    coriolis = CORIOLIS_MAX * jnp.sin(
        jnp.pi * (ids.astype(jnp.float32) + 0.5) / lat_total - 0.5 * jnp.pi
    )
    rows_in = jnp.broadcast_to(jnp.stack([coriolis, inside])[:, :, None], (2, tall, 128))
    angles = np.float32(TWO_PI) * np.arange(sections * STEPS, dtype=np.float32) / np.float32(
        sections * STEPS
    )
    trig = jnp.asarray(np.stack([np.cos(angles), np.sin(angles)], axis=1).reshape(-1))
    f32 = jnp.float32
    dma = pltpu.SemaphoreType.DMA
    any_spec = pl.BlockSpec(memory_space=pl.ANY)
    vmem = pl.BlockSpec(memory_space=pltpu.VMEM)
    stacked = pltpu.VMEM((sections, 3, tall, win), f32)
    plain = pltpu.VMEM((tall, win), f32)
    padded = pltpu.VMEM((tall + 16, win), f32)
    new_fields, mismatch, step = pl.pallas_call(
        functools.partial(kernel, sections, bands, float(sections * 3 * lat_total * lon)),
        out_shape=(
            jax.ShapeDtypeStruct(fields.shape, f32),
            jax.ShapeDtypeStruct(fields.shape, f32),
            jax.ShapeDtypeStruct((8, 128), f32),
        ),
        in_specs=[any_spec] * 5 + [vmem, pl.BlockSpec(memory_space=pltpu.SMEM)],
        out_specs=(vmem, any_spec, vmem),
        scratch_shapes=[
            pltpu.VMEM((3, rows, lon + 2 * SIDE), f32),
            pltpu.VMEM((rows, win), jnp.int32),
            pltpu.VMEM((4, tall, win), f32),
            stacked, stacked, stacked,
            pltpu.VMEM((3, rows, lon), f32),
            plain, plain, plain, padded, padded,
            pltpu.VMEM((2, 8, 128), f32),
            pltpu.VMEM((sections, 2, 8, 128), f32),
            pltpu.VMEM((bands, 2, 8, 128), f32),
            dma((15,)),
            dma((sections,)), dma((sections,)),
            dma((2, sections)), dma((2, sections)),
            dma((2,)), dma((2,)),
            dma((sections,)), dma((sections,)),
            dma((sections,)), dma((sections,)),
            dma((3,)),
            dma((sections,)), dma((sections,)),
            dma((bands,)), dma((bands,)),
        ],
        compiler_params=pltpu.CompilerParams(
            collective_id=0, has_side_effects=True, vmem_limit_bytes=60 * 1024 * 1024
        ),
        name="shooting",
    )(fields, depth_field, land_mask, tide_cos, tide_sin, rows_in, trig)
    return new_fields[None], mismatch[None], step[0, 0]


def solution(mesh):
    return jax.shard_map(
        shards,
        mesh=mesh,
        in_specs=(
            P("sec", None, "lat", None),
            P("lat", None),
            P("lat", None),
            P("lat", None),
            P("lat", None),
        ),
        out_specs=(P("sec", None, "lat", None), P("sec", None, "lat", None), P()),
        check_vma=False,
    )
```

```python
import functools
import math

import jax
import jax.numpy as jnp
import numpy as np
from jax import lax
from jax.experimental import pallas as pl
from jax.experimental.pallas import tpu as pltpu
from jax.sharding import PartitionSpec as P

STEPS = 4
DRAG_RATE = 0.9
CORIOLIS_MAX = 0.3
EPSILON = 1e-06
TWO_PI = 2.0 * math.pi
HALO = 24
MESH = pl.DeviceIdType.MESH


def kernel(
    sections, bands, count,
    states, depth, mask, tide_one, tide_two, rows_in, trig,
    new_states, mismatch, step_out,
    wide, mask_win, st, start, mis, grad, home, full,
    high, east, north, raised, flux, fluy, acc, part, total,
    load_sem, s1, r1, halo_s, halo_r, st_s, st_r, s2, r2, s3, r3, own_sem, ps, pr, ts, tr,
):
    me = lax.axis_index("sec")
    band = lax.axis_index("lat")
    rows, lon = states.shape[1], states.shape[2]
    share = lon // sections
    per, tiles = share // 128, lon // 128
    wins = per + 2
    tall = rows + 2 * HALO
    strips = tall // 8
    top, low = HALO, HALO + rows

    def peer(i):
        return lax.rem(me + i, sections)

    def tile(c):
        return pl.ds(pl.multiple_of(c * 128, 128), 128)

    def load_states(c, _):
        src = states.at[:, :, tile(lax.rem(c + tiles - 1, tiles))]
        pltpu.make_async_copy(src, wide.at[c], load_sem.at[0]).start()
        return 0

    lax.fori_loop(0, tiles + 2, load_states, 0)
    singles = (
        (depth, st.at[0, :, pl.ds(top, rows)]),
        (mask, mask_win),
        (tide_one, st.at[2, :, pl.ds(top, rows)]),
        (tide_two, st.at[3, :, pl.ds(top, rows)]),
    )

    def load_static(c, _):
        at = tile(lax.rem(me * per + c + tiles - 1, tiles))
        for n, (src, dst) in enumerate(singles):
            pltpu.make_async_copy(src.at[:, at], dst.at[c], load_sem.at[1 + n]).start()
        return 0

    lax.fori_loop(0, wins, load_static, 0)

    barrier = pltpu.get_barrier_semaphore()
    for i in range(1, sections):
        pl.semaphore_signal(barrier, inc=1, device_id={"sec": peer(i)}, device_id_type=MESH)
    for i in range(1, bands):
        pl.semaphore_signal(
            barrier, inc=1, device_id={"lat": lax.rem(band + i, bands)}, device_id_type=MESH
        )
    pl.semaphore_wait(barrier, sections + bands - 2)

    pltpu.make_async_copy(wide, wide, load_sem.at[0]).wait()

    def piece(j, slot):
        return pltpu.make_async_remote_copy(
            src_ref=wide.at[pl.ds(j * per, wins)],
            dst_ref=start.at[me, :, :, pl.ds(top, rows), :],
            send_sem=s1.at[j],
            recv_sem=r1.at[slot],
            device_id={"sec": j},
            device_id_type=MESH,
        )

    for i in range(1, sections):
        piece(peer(i), me).start()
    own = pltpu.make_async_copy(
        wide.at[pl.ds(me * per, wins)],
        start.at[me, :, :, pl.ds(top, rows), :],
        own_sem.at[0],
    )
    own.start()

    up_ok, down_ok = band > 0, band < bands - 1

    def to_above(s):
        return pltpu.make_async_remote_copy(
            src_ref=start.at[s, :, :, pl.ds(top, HALO), :],
            dst_ref=start.at[s, :, :, pl.ds(low, HALO), :],
            send_sem=halo_s.at[0, s], recv_sem=halo_r.at[0, s],
            device_id={"lat": band - 1}, device_id_type=MESH,
        )

    def to_below(s):
        return pltpu.make_async_remote_copy(
            src_ref=start.at[s, :, :, pl.ds(low - HALO, HALO), :],
            dst_ref=start.at[s, :, :, pl.ds(0, HALO), :],
            send_sem=halo_s.at[1, s], recv_sem=halo_r.at[1, s],
            device_id={"lat": band + 1}, device_id_type=MESH,
        )

    def st_above():
        return pltpu.make_async_remote_copy(
            src_ref=st.at[:, :, pl.ds(top, HALO), :], dst_ref=st.at[:, :, pl.ds(low, HALO), :],
            send_sem=st_s.at[0], recv_sem=st_r.at[0],
            device_id={"lat": band - 1}, device_id_type=MESH,
        )

    def st_below():
        return pltpu.make_async_remote_copy(
            src_ref=st.at[:, :, pl.ds(low - HALO, HALO), :], dst_ref=st.at[:, :, pl.ds(0, HALO), :],
            send_sem=st_s.at[1], recv_sem=st_r.at[1],
            device_id={"lat": band + 1}, device_id_type=MESH,
        )

    def send_halo(s):
        @pl.when(up_ok)
        def _():
            to_above(s).start()

        @pl.when(down_ok)
        def _():
            to_below(s).start()

    def recv_halo(s):
        @pl.when(down_ok)
        def _():
            to_above(s).wait_recv()

        @pl.when(up_ok)
        def _():
            to_below(s).wait_recv()

    own.wait()
    send_halo(me)

    for n, (src, dst) in enumerate(singles):
        pltpu.make_async_copy(dst, dst, load_sem.at[1 + n]).wait()

    def prepare(r, _):
        at = pl.ds(pl.multiple_of(top + 8 * r, 8), 8)
        for c in range(wins):
            sea = mask_win[c, pl.ds(pl.multiple_of(8 * r, 8), 8), :].astype(jnp.float32)
            st[1, c, at, :] = sea
            st[0, c, at, :] = st[0, c, at, :] * sea
        return 0

    lax.fori_loop(0, rows // 8, prepare, 0)

    @pl.when(up_ok)
    def _():
        st_above().start()

    @pl.when(down_ok)
    def _():
        st_below().start()

    zero = jnp.zeros((8, 128), jnp.float32)

    def blank(first):
        def body(r, _):
            at = pl.ds(pl.multiple_of(first + 8 * r, 8), 8)
            for c in range(wins):
                for a in range(4):
                    st[a, c, at, :] = zero
                for s in range(sections):
                    for a in range(3):
                        start[s, c, a, at, :] = zero
            return 0

        lax.fori_loop(0, HALO // 8, body, 0)

    @pl.when(band == 0)
    def _():
        blank(0)

    @pl.when(band == bands - 1)
    def _():
        blank(low)

    def edge(lo, hi):
        for buf in (raised, flux):
            for c in range(wins):
                buf[c, pl.ds(8 * lo, 8), :] = zero
                buf[c, pl.ds(8 * hi + 8, 8), :] = zero

    acc[...] = jnp.zeros_like(acc)

    @pl.when(down_ok)
    def _():
        st_above().wait_recv()

    @pl.when(up_ok)
    def _():
        st_below().wait_recv()

    lane = lax.broadcasted_iota(jnp.int32, (8, 128), 1)

    def lon_diff(xs, c):
        after, before = xs[min(c + 1, wins - 1)], xs[max(c - 1, 0)]
        east_of = pltpu.roll(jnp.where(lane == 0, after, xs[c]), 127, 1)
        return east_of - pltpu.roll(jnp.where(lane == 127, before, xs[c]), 1, 1)

    def lat_diff(ref, c, r0):
        return ref[c, pl.ds(r0 + 9, 8), :] - ref[c, pl.ds(r0 + 7, 8), :]

    def run(kind, source, s, lo, hi, finish):
        def push(h, c, at, step):
            if kind != "forced":
                return 0.5 * h
            base = 2 * (s * STEPS + step)
            return 0.5 * (h + (trig[base] * st[2, c, at, :] + trig[base + 1] * st[3, c, at, :]))

        def begin(r, _):
            r0 = pl.multiple_of(8 * r, 8)
            at = pl.ds(r0, 8)
            for c in range(wins):
                raised[c, pl.ds(pl.multiple_of(r0 + 8, 8), 8), :] = push(
                    source[s, c, 0, at, :], c, at, 0
                )
            return 0

        lax.fori_loop(lo, hi, begin, 0)
        edge(lo, hi)
        for step in range(STEPS):
            def first(r, _):
                r0 = pl.multiple_of(8 * r, 8)
                at = pl.ds(r0, 8)
                padded = pl.ds(pl.multiple_of(r0 + 8, 8), 8)
                cor = rows_in[0, at, :]
                xs = [raised[c, padded, :] for c in range(wins)]
                for c in range(wins):
                    wet, sea = st[0, c, at, :], st[1, c, at, :]
                    dx, dy = lon_diff(xs, c), lat_diff(raised, c, r0)
                    if step == 0:
                        u, v = source[s, c, 1, at, :], source[s, c, 2, at, :]
                    else:
                        u, v = east[c, at, :], north[c, at, :]
                    if kind == "back":
                        e = sea * (u + wet * dx)
                        f = sea * (v + wet * dy)
                        east[c, at, :] = DRAG_RATE * e - cor * f
                        north[c, at, :] = cor * e + DRAG_RATE * f
                        fluy[c, at, :] = 0.5 * e
                        flux[c, padded, :] = 0.5 * f
                    else:
                        e = sea * (DRAG_RATE * u + cor * v - dx)
                        f = sea * (DRAG_RATE * v - cor * u - dy)
                        east[c, at, :] = e
                        north[c, at, :] = f
                        half = 0.5 * wet
                        fluy[c, at, :] = half * e
                        flux[c, padded, :] = half * f
                return 0

            lax.fori_loop(lo, hi, first, 0)

            def second(r, _):
                r0 = pl.multiple_of(8 * r, 8)
                at = pl.ds(r0, 8)
                inside = rows_in[1, at, :]
                xs = [fluy[c, at, :] for c in range(wins)]
                out = []
                for c in range(wins):
                    d = lon_diff(xs, c) + lat_diff(flux, c, r0)
                    h = source[s, c, 0, at, :] if step == 0 else high[c, at, :]
                    h = (h + d if kind == "back" else h - d) * inside
                    if step == STEPS - 1:
                        out.append(finish(c, at, (h, east[c, at, :], north[c, at, :])))
                    else:
                        high[c, at, :] = h
                        raised[c, pl.ds(pl.multiple_of(r0 + 8, 8), 8), :] = push(
                            h, c, at, step + 1
                        )
                if kind == "free" and step == STEPS - 1:
                    acc[0] += sum(x for x, _ in out[1:-1])
                    acc[1] += sum(x for _, x in out[1:-1])
                return 0

            inner = 1 if step == STEPS - 1 else 0
            lax.fori_loop(lo + inner, hi - inner, second, 0)

    recv_halo(me)

    def keep(c, at, values):
        for a, x in enumerate(values):
            mis[me, c, a, at, :] = x

    run("forced", start, me, 0, strips, keep)

    def arrive(i, _):
        s = peer(i)
        piece(s, s).wait_recv()
        send_halo(s)
        return 0

    lax.fori_loop(1, sections, arrive, 0)

    def arrive_halo(i, _):
        recv_halo(peer(i))
        return 0

    lax.fori_loop(1, sections, arrive_halo, 0)

    def mine(r, _):
        at = pl.ds(pl.multiple_of(8 * r, 8), 8)
        for c in range(wins):
            for a in range(3):
                mis[me, c, a, at, :] = mis[me, c, a, at, :] - start[peer(1), c, a, at, :]
        return 0

    lax.fori_loop(1, strips - 1, mine, 0)
    columns = pl.ds(me * per, per)
    own_mis = pltpu.make_async_copy(
        mis.at[me, pl.ds(1, per), :, pl.ds(top, rows), :],
        home.at[columns],
        own_sem.at[1],
    )
    own_mis.start()

    def give(source, target, send, recv, s, at_columns, slot):
        return pltpu.make_async_remote_copy(
            src_ref=source.at[s, pl.ds(1, per), :, pl.ds(top, rows), :],
            dst_ref=target.at[at_columns],
            send_sem=send.at[s], recv_sem=recv.at[slot],
            device_id={"sec": s}, device_id_type=MESH,
        )

    def forced(i, _):
        s = peer(i)
        after = peer(i + 1)

        def done(c, at, values):
            for a, x in enumerate(values):
                mis[s, c, a, at, :] = x - start[after, c, a, at, :]

        run("forced", start, s, 0, strips, done)
        give(mis, home, s2, r2, s, columns, me).start()
        return 0

    lax.fori_loop(1, sections, forced, 0)

    def back(i, _):
        s = peer(i)
        before = peer(i + sections - 1)

        def done(c, at, values):
            for a, x in enumerate(values):
                grad[s, c, a, at, :] = x - mis[before, c, a, at, :]

        run("back", mis, s, 1, strips - 1, done)

        @pl.when(i < sections)
        def _():
            give(grad, full, s3, r3, s, columns, me).start()

        return 0

    lax.fori_loop(1, sections + 1, back, 0)
    own_grad = pltpu.make_async_copy(
        grad.at[me, pl.ds(1, per), :, pl.ds(top, rows), :],
        full.at[columns],
        own_sem.at[2],
    )
    own_grad.start()

    def image(i, _):
        s = peer(i)
        after = peer(i + 1)

        def squares(c, at, values):
            pairs = [(x, grad[after, c, a, at, :]) for a, x in enumerate(values)]
            return sum(g * g for _, g in pairs), sum((x - g) * (x - g) for x, g in pairs)

        run("free", grad, s, 2, strips - 2, squares)
        return 0

    lax.fori_loop(0, sections, image, 0)

    part[me] = acc[...]

    def share_part(j, slot):
        return pltpu.make_async_remote_copy(
            src_ref=acc, dst_ref=part.at[slot], send_sem=ps.at[j], recv_sem=pr.at[slot],
            device_id={"sec": j}, device_id_type=MESH,
        )

    for i in range(1, sections):
        share_part(peer(i), me).start()
    for i in range(1, sections):
        share_part(peer(i), peer(i)).wait_recv()
    for i in range(1, sections):
        share_part(peer(i), me).wait_send()
    summed = part[0]
    for s in range(1, sections):
        summed = summed + part[s]
    acc[...] = summed
    total[band] = summed

    def share_total(j, slot):
        return pltpu.make_async_remote_copy(
            src_ref=acc, dst_ref=total.at[slot], send_sem=ts.at[j], recv_sem=tr.at[slot],
            device_id={"lat": j}, device_id_type=MESH,
        )

    for i in range(1, bands):
        share_total(lax.rem(band + i, bands), band).start()
    for i in range(1, bands):
        j = lax.rem(band + i, bands)
        share_total(j, j).wait_recv()
    summed = total[0]
    for s in range(1, bands):
        summed = summed + total[s]
    sums = jnp.sum(jnp.sum(summed, axis=2, keepdims=True), axis=1, keepdims=True)
    step = sums[0] / count / (sums[1] / count + EPSILON)
    step_out[...] = jnp.broadcast_to(step, (8, 128))

    own_mis.wait()

    def mismatches(i, _):
        s = peer(i)
        give(mis, home, s2, r2, s, columns, s).wait()
        return 0

    lax.fori_loop(1, sections, mismatches, 0)

    def write_out(c, _):
        pltpu.make_async_copy(home.at[c], mismatch.at[:, :, tile(c)], load_sem.at[5]).start()
        return 0

    lax.fori_loop(0, tiles, write_out, 0)
    own_grad.wait()

    def grads(i, _):
        s = peer(i)
        give(grad, full, s3, r3, s, columns, s).wait_recv()
        return 0

    lax.fori_loop(1, sections, grads, 0)

    def update(r, _):
        at = pl.ds(pl.multiple_of(8 * r, 8), 8)
        for c in range(tiles):
            for a in range(3):
                new_states[a, at, c * 128:c * 128 + 128] = (
                    wide[c + 1, a, at, :] - step * full[c, a, at, :]
                )
        return 0

    lax.fori_loop(0, rows // 8, update, 0)

    pltpu.make_async_copy(home, home, load_sem.at[5]).wait()

    def drain(i, _):
        s = peer(i)
        piece(s, me).wait_send()
        give(grad, full, s3, r3, s, columns, me).wait_send()
        return 0

    lax.fori_loop(1, sections, drain, 0)

    def drain_halo(i, _):
        s = peer(i)

        @pl.when(up_ok)
        def _():
            to_above(s).wait_send()

        @pl.when(down_ok)
        def _():
            to_below(s).wait_send()

        return 0

    lax.fori_loop(0, sections, drain_halo, 0)

    @pl.when(up_ok)
    def _():
        st_above().wait_send()

    @pl.when(down_ok)
    def _():
        st_below().wait_send()

    for i in range(1, bands):
        share_total(lax.rem(band + i, bands), band).wait_send()


def shards(states, depth_field, land_mask, tide_cos, tide_sin):
    fields = states[0]
    rows, lon = fields.shape[1:]
    sections, bands = lax.axis_size("sec"), lax.axis_size("lat")
    band = lax.axis_index("lat")
    share = lon // sections
    tall = rows + 2 * HALO
    lat_total = rows * bands
    ids = band * rows - HALO + jnp.arange(tall, dtype=jnp.int32)
    inside = ((ids >= 0) & (ids < lat_total)).astype(jnp.float32)
    coriolis = CORIOLIS_MAX * jnp.sin(
        jnp.pi * (ids.astype(jnp.float32) + 0.5) / lat_total - 0.5 * jnp.pi
    )
    rows_in = jnp.broadcast_to(jnp.stack([coriolis, inside])[:, :, None], (2, tall, 128))
    angles = np.float32(TWO_PI) * np.arange(sections * STEPS, dtype=np.float32) / np.float32(
        sections * STEPS
    )
    trig = jnp.asarray(np.stack([np.cos(angles), np.sin(angles)], axis=1).reshape(-1))
    f32 = jnp.float32
    dma = pltpu.SemaphoreType.DMA
    any_spec = pl.BlockSpec(memory_space=pl.ANY)
    vmem = pl.BlockSpec(memory_space=pltpu.VMEM)
    tiles, wins = lon // 128, share // 128 + 2
    stacked = pltpu.VMEM((sections, wins, 3, tall, 128), f32)
    plain = pltpu.VMEM((wins, tall, 128), f32)
    padded = pltpu.VMEM((wins, tall + 16, 128), f32)
    gathered = pltpu.VMEM((tiles, 3, rows, 128), f32)
    new_fields, mismatch, step = pl.pallas_call(
        functools.partial(kernel, sections, bands, float(sections * 3 * lat_total * lon)),
        out_shape=(
            jax.ShapeDtypeStruct(fields.shape, f32),
            jax.ShapeDtypeStruct(fields.shape, f32),
            jax.ShapeDtypeStruct((8, 128), f32),
        ),
        in_specs=[any_spec] * 5 + [vmem, pl.BlockSpec(memory_space=pltpu.SMEM)],
        out_specs=(vmem, any_spec, vmem),
        scratch_shapes=[
            pltpu.VMEM((tiles + 2, 3, rows, 128), f32),
            pltpu.VMEM((wins, rows, 128), jnp.int32),
            pltpu.VMEM((4, wins, tall, 128), f32),
            stacked, stacked, stacked,
            gathered, gathered,
            plain, plain, plain, padded, padded, plain,
            pltpu.VMEM((2, 8, 128), f32),
            pltpu.VMEM((sections, 2, 8, 128), f32),
            pltpu.VMEM((bands, 2, 8, 128), f32),
            dma((6,)),
            dma((sections,)), dma((sections,)),
            dma((2, sections)), dma((2, sections)),
            dma((2,)), dma((2,)),
            dma((sections,)), dma((sections,)),
            dma((sections,)), dma((sections,)),
            dma((3,)),
            dma((sections,)), dma((sections,)),
            dma((bands,)), dma((bands,)),
        ],
        compiler_params=pltpu.CompilerParams(
            collective_id=0, has_side_effects=True, vmem_limit_bytes=60 * 1024 * 1024
        ),
        name="shooting",
    )(fields, depth_field, land_mask, tide_cos, tide_sin, rows_in, trig)
    return new_fields[None], mismatch[None], step[0, 0]


def solution(mesh):
    return jax.shard_map(
        shards,
        mesh=mesh,
        in_specs=(
            P("sec", None, "lat", None),
            P("lat", None),
            P("lat", None),
            P("lat", None),
            P("lat", None),
        ),
        out_specs=(P("sec", None, "lat", None), P("sec", None, "lat", None), P()),
        check_vma=False,
    )
```

```python
import functools
import math

import jax
import jax.numpy as jnp
import numpy as np
from jax import lax
from jax.experimental import pallas as pl
from jax.experimental.pallas import tpu as pltpu
from jax.sharding import PartitionSpec as P

STEPS = 4
DRAG_RATE = 0.9
CORIOLIS_MAX = 0.3
EPSILON = 1e-06
TWO_PI = 2.0 * math.pi
HALO = 24
MESH = pl.DeviceIdType.MESH


def kernel(
    sections, bands, count,
    states, depth, mask, tide_one, tide_two, rows_in, trig,
    home, full, step_out,
    wide, mask_win, st, start, mis, grad,
    high, east, north, raised, flux, fluy, acc, part, total,
    load_sem, s1, r1, halo_s, halo_r, st_s, st_r, s2, r2, s3, r3, own_sem, ps, pr, ts, tr,
):
    me = lax.axis_index("sec")
    band = lax.axis_index("lat")
    rows, lon = states.shape[1], states.shape[2]
    share = lon // sections
    per, tiles = share // 128, lon // 128
    wins = per + 1
    tall = rows + 2 * HALO
    strips = tall // 8
    top, low = HALO, HALO + rows

    def peer(i):
        return lax.rem(me + i, sections)

    def tile(c):
        return pl.ds(pl.multiple_of(c * 128, 128), 128)

    def load_states(c, _):
        src = states.at[:, :, tile(c)]
        pltpu.make_async_copy(src, wide.at[c + c // per], load_sem.at[0]).start()
        return 0

    lax.fori_loop(0, tiles, load_states, 0)
    singles = (
        (depth, st.at[0, :, pl.ds(top, rows)]),
        (mask, mask_win),
        (tide_one, st.at[2, :, pl.ds(top, rows)]),
        (tide_two, st.at[3, :, pl.ds(top, rows)]),
    )

    def load_static(c, _):
        ahead = jnp.where(c == wins, tiles - 1, c)
        at = tile(lax.rem(me * per + ahead, tiles))
        for n, (src, dst) in enumerate(singles):
            pltpu.make_async_copy(src.at[:, at], dst.at[c], load_sem.at[1 + n]).start()
        return 0

    lax.fori_loop(0, wins + 1, load_static, 0)

    barrier = pltpu.get_barrier_semaphore()
    for i in range(1, sections):
        pl.semaphore_signal(barrier, inc=1, device_id={"sec": peer(i)}, device_id_type=MESH)
    for i in range(1, bands):
        pl.semaphore_signal(
            barrier, inc=1, device_id={"lat": lax.rem(band + i, bands)}, device_id_type=MESH
        )
    pl.semaphore_wait(barrier, sections + bands - 2)

    loaded = wide.at[pl.ds(0, tiles)]
    pltpu.make_async_copy(loaded, loaded, load_sem.at[0]).wait()
    early = lax.broadcasted_iota(jnp.int32, (8, 128), 1) < 64

    def pack(r, _):
        at = pl.ds(pl.multiple_of(8 * r, 8), 8)
        for j in range(sections):
            after, before = (j + 1) % sections * wins, (j - 1) % sections * wins + per - 1
            for a in range(3):
                wide[j * wins + per, a, at, :] = jnp.where(
                    early, wide[after, a, at, :], wide[before, a, at, :]
                )
        return 0

    lax.fori_loop(0, rows // 8, pack, 0)

    def piece(j, slot):
        return pltpu.make_async_remote_copy(
            src_ref=wide.at[pl.ds(j * wins, wins)],
            dst_ref=start.at[me, :, :, pl.ds(top, rows), :],
            send_sem=s1.at[j],
            recv_sem=r1.at[slot],
            device_id={"sec": j},
            device_id_type=MESH,
        )

    for i in range(1, sections):
        piece(peer(i), me).start()
    own = pltpu.make_async_copy(
        wide.at[pl.ds(me * wins, wins)],
        start.at[me, :, :, pl.ds(top, rows), :],
        own_sem.at[0],
    )
    own.start()

    up_ok, down_ok = band > 0, band < bands - 1

    def to_above(s):
        return pltpu.make_async_remote_copy(
            src_ref=start.at[s, :, :, pl.ds(top, HALO), :],
            dst_ref=start.at[s, :, :, pl.ds(low, HALO), :],
            send_sem=halo_s.at[0, s], recv_sem=halo_r.at[0, s],
            device_id={"lat": band - 1}, device_id_type=MESH,
        )

    def to_below(s):
        return pltpu.make_async_remote_copy(
            src_ref=start.at[s, :, :, pl.ds(low - HALO, HALO), :],
            dst_ref=start.at[s, :, :, pl.ds(0, HALO), :],
            send_sem=halo_s.at[1, s], recv_sem=halo_r.at[1, s],
            device_id={"lat": band + 1}, device_id_type=MESH,
        )

    def st_above():
        return pltpu.make_async_remote_copy(
            src_ref=st.at[:, pl.ds(0, wins), pl.ds(top, HALO), :], dst_ref=st.at[:, pl.ds(0, wins), pl.ds(low, HALO), :],
            send_sem=st_s.at[0], recv_sem=st_r.at[0],
            device_id={"lat": band - 1}, device_id_type=MESH,
        )

    def st_below():
        return pltpu.make_async_remote_copy(
            src_ref=st.at[:, pl.ds(0, wins), pl.ds(low - HALO, HALO), :], dst_ref=st.at[:, pl.ds(0, wins), pl.ds(0, HALO), :],
            send_sem=st_s.at[1], recv_sem=st_r.at[1],
            device_id={"lat": band + 1}, device_id_type=MESH,
        )

    def send_halo(s):
        @pl.when(up_ok)
        def _():
            to_above(s).start()

        @pl.when(down_ok)
        def _():
            to_below(s).start()

    def recv_halo(s):
        @pl.when(down_ok)
        def _():
            to_above(s).wait_recv()

        @pl.when(up_ok)
        def _():
            to_below(s).wait_recv()

    own.wait()
    send_halo(me)

    for n, (src, dst) in enumerate(singles):
        pltpu.make_async_copy(dst, dst, load_sem.at[1 + n]).wait()

    def prepare(r, _):
        at = pl.ds(pl.multiple_of(top + 8 * r, 8), 8)
        for c in range(wins + 1):
            sea = mask_win[c, pl.ds(pl.multiple_of(8 * r, 8), 8), :].astype(jnp.float32)
            st[1, c, at, :] = sea
            st[0, c, at, :] = st[0, c, at, :] * sea
        for a in range(4):
            st[a, per, at, :] = jnp.where(early, st[a, per, at, :], st[a, wins, at, :])
        return 0

    lax.fori_loop(0, rows // 8, prepare, 0)

    @pl.when(up_ok)
    def _():
        st_above().start()

    @pl.when(down_ok)
    def _():
        st_below().start()

    zero = jnp.zeros((8, 128), jnp.float32)

    def blank(first):
        def body(r, _):
            at = pl.ds(pl.multiple_of(first + 8 * r, 8), 8)
            for c in range(wins):
                for a in range(4):
                    st[a, c, at, :] = zero
                for s in range(sections):
                    for a in range(3):
                        start[s, c, a, at, :] = zero
            return 0

        lax.fori_loop(0, HALO // 8, body, 0)

    @pl.when(band == 0)
    def _():
        blank(0)

    @pl.when(band == bands - 1)
    def _():
        blank(low)

    def edge(lo, hi):
        for buf in (raised, flux):
            for c in range(wins):
                buf[c, pl.ds(8 * lo, 8), :] = zero
                buf[c, pl.ds(8 * hi + 8, 8), :] = zero

    acc[...] = jnp.zeros_like(acc)

    @pl.when(down_ok)
    def _():
        st_above().wait_recv()

    @pl.when(up_ok)
    def _():
        st_below().wait_recv()

    lane = lax.broadcasted_iota(jnp.int32, (8, 128), 1)

    def lon_diff(xs, c):
        after, before = xs[(c + 1) % wins], xs[c - 1]
        east_of = pltpu.roll(jnp.where(lane == 0, after, xs[c]), 127, 1)
        return east_of - pltpu.roll(jnp.where(lane == 127, before, xs[c]), 1, 1)

    def lat_diff(ref, c, r0):
        return ref[c, pl.ds(r0 + 9, 8), :] - ref[c, pl.ds(r0 + 7, 8), :]

    def run(kind, source, s, lo, hi, finish, target_of=None):
        def push(h, c, at, step):
            if kind != "forced":
                return 0.5 * h
            base = 2 * (s * STEPS + step)
            return 0.5 * (h + (trig[base] * st[2, c, at, :] + trig[base + 1] * st[3, c, at, :]))

        def begin(r, _):
            r0 = pl.multiple_of(8 * r, 8)
            at = pl.ds(r0, 8)
            for c in range(wins):
                raised[c, pl.ds(pl.multiple_of(r0 + 8, 8), 8), :] = push(
                    source[s, c, 0, at, :], c, at, 0
                )
            return 0

        lax.fori_loop(lo, hi, begin, 0)
        edge(lo, hi)
        for step in range(STEPS):
            def first(r, _):
                r0 = pl.multiple_of(8 * r, 8)
                at = pl.ds(r0, 8)
                padded = pl.ds(pl.multiple_of(r0 + 8, 8), 8)
                cor = rows_in[0, at, :]
                xs = [raised[c, padded, :] for c in range(wins)]
                out = []
                for c in range(wins):
                    wet, sea = st[0, c, at, :], st[1, c, at, :]
                    dx, dy = lon_diff(xs, c), lat_diff(raised, c, r0)
                    if step == 0:
                        u, v = source[s, c, 1, at, :], source[s, c, 2, at, :]
                    else:
                        u, v = east[c, at, :], north[c, at, :]
                    if kind == "back":
                        e = sea * (u + wet * dx)
                        f = sea * (v + wet * dy)
                        out.append((
                            DRAG_RATE * e - cor * f, cor * e + DRAG_RATE * f, 0.5 * e, 0.5 * f
                        ))
                    else:
                        e = sea * (DRAG_RATE * u + cor * v - dx)
                        f = sea * (DRAG_RATE * v - cor * u - dy)
                        half = 0.5 * wet
                        out.append((e, f, half * e, half * f))
                for c in range(wins):
                    east[c, at, :], north[c, at, :] = out[c][0], out[c][1]
                    fluy[c, at, :], flux[c, padded, :] = out[c][2], out[c][3]
                return 0

            lax.fori_loop(lo, hi, first, 0)

            def second(r, _):
                r0 = pl.multiple_of(8 * r, 8)
                at = pl.ds(r0, 8)
                inside = rows_in[1, at, :]
                xs = [fluy[c, at, :] for c in range(wins)]
                out = []
                for c in range(wins):
                    d = lon_diff(xs, c) + lat_diff(flux, c, r0)
                    h = source[s, c, 0, at, :] if step == 0 else high[c, at, :]
                    h = (h + d if kind == "back" else h - d) * inside
                    if step == STEPS - 1:
                        out.append(finish(c, at, (h, east[c, at, :], north[c, at, :])))
                    else:
                        out.append((h, push(h, c, at, step + 1)))
                if step < STEPS - 1:
                    ahead = pl.ds(pl.multiple_of(r0 + 8, 8), 8)
                    for c in range(wins):
                        high[c, at, :], raised[c, ahead, :] = out[c]
                elif kind == "free":
                    acc[0] += sum(x for x, _ in out[:-1])
                    acc[1] += sum(x for _, x in out[:-1])
                else:
                    target, slot = target_of
                    for c in range(wins):
                        for a in range(3):
                            target[slot, c, a, at, :] = out[c][a]
                return 0

            inner = 1 if step == STEPS - 1 else 0
            lax.fori_loop(lo + inner, hi - inner, second, 0)

    recv_halo(me)

    def keep(c, at, values):
        return values

    run("forced", start, me, 0, strips, keep, (mis, me))

    def arrive(i, _):
        s = peer(i)
        piece(s, s).wait_recv()
        send_halo(s)
        return 0

    lax.fori_loop(1, sections, arrive, 0)

    def arrive_halo(i, _):
        recv_halo(peer(i))
        return 0

    lax.fori_loop(1, sections, arrive_halo, 0)

    def mine(r, _):
        at = pl.ds(pl.multiple_of(8 * r, 8), 8)
        for c in range(wins):
            for a in range(3):
                mis[me, c, a, at, :] = mis[me, c, a, at, :] - start[peer(1), c, a, at, :]
        return 0

    lax.fori_loop(1, strips - 1, mine, 0)
    columns = pl.ds(me * per, per)
    own_mis = pltpu.make_async_copy(
        mis.at[me, pl.ds(0, per), :, pl.ds(top, rows), :],
        home.at[columns],
        own_sem.at[1],
    )
    own_mis.start()

    def give(source, target, send, recv, s, at_columns, slot):
        return pltpu.make_async_remote_copy(
            src_ref=source.at[s, pl.ds(0, per), :, pl.ds(top, rows), :],
            dst_ref=target.at[at_columns],
            send_sem=send.at[s], recv_sem=recv.at[slot],
            device_id={"sec": s}, device_id_type=MESH,
        )

    def forced(i, _):
        s = peer(i)
        after = peer(i + 1)

        def done(c, at, values):
            return [x - start[after, c, a, at, :] for a, x in enumerate(values)]

        run("forced", start, s, 0, strips, done, (mis, s))
        give(mis, home, s2, r2, s, columns, me).start()
        return 0

    lax.fori_loop(1, sections, forced, 0)

    def back(i, _):
        s = peer(i)
        before = peer(i + sections - 1)

        def done(c, at, values):
            return [x - mis[before, c, a, at, :] for a, x in enumerate(values)]

        run("back", mis, s, 1, strips - 1, done, (grad, s))

        @pl.when(i < sections)
        def _():
            give(grad, full, s3, r3, s, columns, me).start()

        return 0

    lax.fori_loop(1, sections + 1, back, 0)
    own_grad = pltpu.make_async_copy(
        grad.at[me, pl.ds(0, per), :, pl.ds(top, rows), :],
        full.at[columns],
        own_sem.at[2],
    )
    own_grad.start()

    def image(i, _):
        s = peer(i)
        after = peer(i + 1)

        def squares(c, at, values):
            pairs = [(x, grad[after, c, a, at, :]) for a, x in enumerate(values)]
            return sum(g * g for _, g in pairs), sum((x - g) * (x - g) for x, g in pairs)

        run("free", grad, s, 2, strips - 2, squares)
        return 0

    lax.fori_loop(0, sections, image, 0)

    part[me] = acc[...]

    def share_part(j, slot):
        return pltpu.make_async_remote_copy(
            src_ref=acc, dst_ref=part.at[slot], send_sem=ps.at[j], recv_sem=pr.at[slot],
            device_id={"sec": j}, device_id_type=MESH,
        )

    for i in range(1, sections):
        share_part(peer(i), me).start()
    for i in range(1, sections):
        share_part(peer(i), peer(i)).wait_recv()
    for i in range(1, sections):
        share_part(peer(i), me).wait_send()
    summed = part[0]
    for s in range(1, sections):
        summed = summed + part[s]
    acc[...] = summed
    total[band] = summed

    def share_total(j, slot):
        return pltpu.make_async_remote_copy(
            src_ref=acc, dst_ref=total.at[slot], send_sem=ts.at[j], recv_sem=tr.at[slot],
            device_id={"lat": j}, device_id_type=MESH,
        )

    for i in range(1, bands):
        share_total(lax.rem(band + i, bands), band).start()
    for i in range(1, bands):
        j = lax.rem(band + i, bands)
        share_total(j, j).wait_recv()
    summed = total[0]
    for s in range(1, bands):
        summed = summed + total[s]
    sums = jnp.sum(jnp.sum(summed, axis=2, keepdims=True), axis=1, keepdims=True)
    step = sums[0] / count / (sums[1] / count + EPSILON)
    step_out[...] = jnp.broadcast_to(step, (8, 128))

    own_mis.wait()

    def mismatches(i, _):
        s = peer(i)
        give(mis, home, s2, r2, s, columns, s).wait()
        return 0

    lax.fori_loop(1, sections, mismatches, 0)

    own_grad.wait()

    def grads(i, _):
        s = peer(i)
        give(grad, full, s3, r3, s, columns, s).wait_recv()
        return 0

    lax.fori_loop(1, sections, grads, 0)


    def drain(i, _):
        s = peer(i)
        piece(s, me).wait_send()
        give(grad, full, s3, r3, s, columns, me).wait_send()
        return 0

    lax.fori_loop(1, sections, drain, 0)

    def drain_halo(i, _):
        s = peer(i)

        @pl.when(up_ok)
        def _():
            to_above(s).wait_send()

        @pl.when(down_ok)
        def _():
            to_below(s).wait_send()

        return 0

    lax.fori_loop(0, sections, drain_halo, 0)

    @pl.when(up_ok)
    def _():
        st_above().wait_send()

    @pl.when(down_ok)
    def _():
        st_below().wait_send()

    for i in range(1, bands):
        share_total(lax.rem(band + i, bands), band).wait_send()


def finish_kernel(fields, home, full, step, new_fields, mismatch):
    rows, share = fields.shape[1:]
    length = step[0:1, :]

    def body(r, _):
        at = pl.ds(pl.multiple_of(8 * r, 8), 8)
        for c in range(share // 128):
            cols = slice(c * 128, c * 128 + 128)
            for a in range(3):
                new_fields[a, at, cols] = fields[a, at, cols] - length * full[c, a, at, :]
                mismatch[a, at, cols] = home[c, a, at, :]
        return 0

    lax.fori_loop(0, rows // 8, body, 0)


def shards(states, depth_field, land_mask, tide_cos, tide_sin):
    fields = states[0]
    rows, lon = fields.shape[1:]
    sections, bands = lax.axis_size("sec"), lax.axis_size("lat")
    band = lax.axis_index("lat")
    share = lon // sections
    tall = rows + 2 * HALO
    lat_total = rows * bands
    ids = band * rows - HALO + jnp.arange(tall, dtype=jnp.int32)
    inside = ((ids >= 0) & (ids < lat_total)).astype(jnp.float32)
    coriolis = CORIOLIS_MAX * jnp.sin(
        jnp.pi * (ids.astype(jnp.float32) + 0.5) / lat_total - 0.5 * jnp.pi
    )
    rows_in = jnp.broadcast_to(jnp.stack([coriolis, inside])[:, :, None], (2, tall, 128))
    angles = np.float32(TWO_PI) * np.arange(sections * STEPS, dtype=np.float32) / np.float32(
        sections * STEPS
    )
    trig = jnp.asarray(np.stack([np.cos(angles), np.sin(angles)], axis=1).reshape(-1))
    f32 = jnp.float32
    dma = pltpu.SemaphoreType.DMA
    any_spec = pl.BlockSpec(memory_space=pl.ANY)
    vmem = pl.BlockSpec(memory_space=pltpu.VMEM)
    tiles, wins = lon // 128, share // 128 + 1
    stacked = pltpu.VMEM((sections, wins, 3, tall, 128), f32)
    plain = pltpu.VMEM((wins, tall, 128), f32)
    padded = pltpu.VMEM((wins, tall + 16, 128), f32)
    gathered = jax.ShapeDtypeStruct((tiles, 3, rows, 128), f32)
    home, full, step = pl.pallas_call(
        functools.partial(kernel, sections, bands, float(sections * 3 * lat_total * lon)),
        out_shape=(
            gathered,
            gathered,
            jax.ShapeDtypeStruct((8, 128), f32),
        ),
        in_specs=[any_spec] * 5 + [vmem, pl.BlockSpec(memory_space=pltpu.SMEM)],
        out_specs=(any_spec, any_spec, vmem),
        scratch_shapes=[
            pltpu.VMEM((tiles + sections, 3, rows, 128), f32),
            pltpu.VMEM((wins + 1, rows, 128), jnp.int32),
            pltpu.VMEM((4, wins + 1, tall, 128), f32),
            stacked, stacked, stacked,
            plain, plain, plain, padded, padded, plain,
            pltpu.VMEM((2, 8, 128), f32),
            pltpu.VMEM((sections, 2, 8, 128), f32),
            pltpu.VMEM((bands, 2, 8, 128), f32),
            dma((5,)),
            dma((sections,)), dma((sections,)),
            dma((2, sections)), dma((2, sections)),
            dma((2,)), dma((2,)),
            dma((sections,)), dma((sections,)),
            dma((sections,)), dma((sections,)),
            dma((3,)),
            dma((sections,)), dma((sections,)),
            dma((bands,)), dma((bands,)),
        ],
        compiler_params=pltpu.CompilerParams(
            collective_id=0, has_side_effects=True, vmem_limit_bytes=60 * 1024 * 1024
        ),
        name="shooting",
    )(fields, depth_field, land_mask, tide_cos, tide_sin, rows_in, trig)
    block = pl.BlockSpec((3, rows, share), lambda i: (0, 0, i))
    by_tile = pl.BlockSpec((share // 128, 3, rows, 128), lambda i: (i, 0, 0, 0))
    new_fields, mismatch = pl.pallas_call(
        finish_kernel,
        grid=(sections,),
        out_shape=(jax.ShapeDtypeStruct(fields.shape, f32),) * 2,
        in_specs=[block, by_tile, by_tile, pl.BlockSpec((8, 128), lambda i: (0, 0))],
        out_specs=(block, block),
        compiler_params=pltpu.CompilerParams(vmem_limit_bytes=32 * 1024 * 1024),
        name="update",
    )(fields, home, full, step)
    return new_fields[None], mismatch[None], step[0, 0]


def solution(mesh):
    return jax.shard_map(
        shards,
        mesh=mesh,
        in_specs=(
            P("sec", None, "lat", None),
            P("lat", None),
            P("lat", None),
            P("lat", None),
            P("lat", None),
        ),
        out_specs=(P("sec", None, "lat", None), P("sec", None, "lat", None), P()),
        check_vma=False,
    )
```

```python
import functools
import math

import jax
import jax.numpy as jnp
import numpy as np
from jax import lax
from jax.experimental import pallas as pl
from jax.experimental.pallas import tpu as pltpu
from jax.sharding import PartitionSpec as P

STEPS = 4
DRAG_RATE = 0.9
CORIOLIS_MAX = 0.3
EPSILON = 1e-06
TWO_PI = 2.0 * math.pi
HALO = 24
MESH = pl.DeviceIdType.MESH


def kernel(
    sections, bands, count,
    states, depth, mask, tide_one, tide_two, rows_in, trig,
    home, full, step_out,
    wide, mask_win, st, start, mis, grad,
    high, east, north, raised, flux, fluy, acc, part, total,
    load_sem, s1, r1, halo_s, halo_r, st_s, st_r, s2, r2, s3, r3, own_sem, ps, pr, ts, tr,
):
    me = lax.axis_index("sec")
    band = lax.axis_index("lat")
    rows, lon = states.shape[1], states.shape[2]
    share = lon // sections
    per, tiles = share // 128, lon // 128
    wins = per + 1
    tall = rows + 2 * HALO
    strips = tall // 8
    top, low = HALO, HALO + rows

    def peer(i):
        return lax.rem(me + i, sections)

    def tile(c):
        return pl.ds(pl.multiple_of(c * 128, 128), 128)

    def load_states(c, _):
        src = states.at[:, :, tile(c)]
        pltpu.make_async_copy(src, wide.at[c + c // per], load_sem.at[0]).start()
        return 0

    lax.fori_loop(0, tiles, load_states, 0)
    singles = (
        (depth, st.at[0, :, pl.ds(top, rows)]),
        (mask, mask_win),
        (tide_one, st.at[2, :, pl.ds(top, rows)]),
        (tide_two, st.at[3, :, pl.ds(top, rows)]),
    )

    def load_static(c, _):
        ahead = jnp.where(c == wins, tiles - 1, c)
        at = tile(lax.rem(me * per + ahead, tiles))
        for n, (src, dst) in enumerate(singles):
            pltpu.make_async_copy(src.at[:, at], dst.at[c], load_sem.at[1 + n]).start()
        return 0

    lax.fori_loop(0, wins + 1, load_static, 0)

    barrier = pltpu.get_barrier_semaphore()
    for i in range(1, sections):
        pl.semaphore_signal(barrier, inc=1, device_id={"sec": peer(i)}, device_id_type=MESH)
    for i in range(1, bands):
        pl.semaphore_signal(
            barrier, inc=1, device_id={"lat": lax.rem(band + i, bands)}, device_id_type=MESH
        )
    pl.semaphore_wait(barrier, sections + bands - 2)

    loaded = wide.at[pl.ds(0, tiles)]
    pltpu.make_async_copy(loaded, loaded, load_sem.at[0]).wait()
    early = lax.broadcasted_iota(jnp.int32, (8, 128), 1) < 64

    def pack(r, _):
        at = pl.ds(pl.multiple_of(8 * r, 8), 8)
        for j in range(sections):
            after, before = (j + 1) % sections * wins, (j - 1) % sections * wins + per - 1
            for a in range(3):
                wide[j * wins + per, a, at, :] = jnp.where(
                    early, wide[after, a, at, :], wide[before, a, at, :]
                )
        return 0

    lax.fori_loop(0, rows // 8, pack, 0)

    def piece(j, slot):
        return pltpu.make_async_remote_copy(
            src_ref=wide.at[pl.ds(j * wins, wins)],
            dst_ref=start.at[me, :, :, pl.ds(top, rows), :],
            send_sem=s1.at[j],
            recv_sem=r1.at[slot],
            device_id={"sec": j},
            device_id_type=MESH,
        )

    def turn(n):
        return lax.rem(me + jnp.where(lax.rem(me, 2) == 0, n, sections - n), sections)

    for n in range(1, sections - 1):
        piece(turn(n), me).start()
    own = pltpu.make_async_copy(
        wide.at[pl.ds(me * wins, wins)],
        start.at[me, :, :, pl.ds(top, rows), :],
        own_sem.at[0],
    )
    own.start()

    up_ok, down_ok = band > 0, band < bands - 1

    def to_above(s):
        return pltpu.make_async_remote_copy(
            src_ref=start.at[s, :, :, pl.ds(top, HALO), :],
            dst_ref=start.at[s, :, :, pl.ds(low, HALO), :],
            send_sem=halo_s.at[0, s], recv_sem=halo_r.at[0, s],
            device_id={"lat": band - 1}, device_id_type=MESH,
        )

    def to_below(s):
        return pltpu.make_async_remote_copy(
            src_ref=start.at[s, :, :, pl.ds(low - HALO, HALO), :],
            dst_ref=start.at[s, :, :, pl.ds(0, HALO), :],
            send_sem=halo_s.at[1, s], recv_sem=halo_r.at[1, s],
            device_id={"lat": band + 1}, device_id_type=MESH,
        )

    def st_above():
        return pltpu.make_async_remote_copy(
            src_ref=st.at[:, pl.ds(0, wins), pl.ds(top, HALO), :], dst_ref=st.at[:, pl.ds(0, wins), pl.ds(low, HALO), :],
            send_sem=st_s.at[0], recv_sem=st_r.at[0],
            device_id={"lat": band - 1}, device_id_type=MESH,
        )

    def st_below():
        return pltpu.make_async_remote_copy(
            src_ref=st.at[:, pl.ds(0, wins), pl.ds(low - HALO, HALO), :], dst_ref=st.at[:, pl.ds(0, wins), pl.ds(0, HALO), :],
            send_sem=st_s.at[1], recv_sem=st_r.at[1],
            device_id={"lat": band + 1}, device_id_type=MESH,
        )

    def send_halo(s):
        @pl.when(up_ok)
        def _():
            to_above(s).start()

        @pl.when(down_ok)
        def _():
            to_below(s).start()

    def recv_halo(s):
        @pl.when(down_ok)
        def _():
            to_above(s).wait_recv()

        @pl.when(up_ok)
        def _():
            to_below(s).wait_recv()

    own.wait()
    send_halo(me)

    for n, (src, dst) in enumerate(singles):
        pltpu.make_async_copy(dst, dst, load_sem.at[1 + n]).wait()

    def prepare(r, _):
        at = pl.ds(pl.multiple_of(top + 8 * r, 8), 8)
        for c in range(wins + 1):
            sea = mask_win[c, pl.ds(pl.multiple_of(8 * r, 8), 8), :].astype(jnp.float32)
            st[1, c, at, :] = sea
            st[0, c, at, :] = st[0, c, at, :] * sea
        for a in range(4):
            st[a, per, at, :] = jnp.where(early, st[a, per, at, :], st[a, wins, at, :])
        return 0

    lax.fori_loop(0, rows // 8, prepare, 0)

    @pl.when(up_ok)
    def _():
        st_above().start()

    @pl.when(down_ok)
    def _():
        st_below().start()

    zero = jnp.zeros((8, 128), jnp.float32)

    def blank(first):
        def body(r, _):
            at = pl.ds(pl.multiple_of(first + 8 * r, 8), 8)
            for c in range(wins):
                for a in range(4):
                    st[a, c, at, :] = zero
                for s in range(sections):
                    for a in range(3):
                        start[s, c, a, at, :] = zero
            return 0

        lax.fori_loop(0, HALO // 8, body, 0)

    @pl.when(band == 0)
    def _():
        blank(0)

    @pl.when(band == bands - 1)
    def _():
        blank(low)

    def edge(lo, hi):
        for buf in (raised, flux):
            for c in range(wins):
                buf[c, pl.ds(8 * lo, 8), :] = zero
                buf[c, pl.ds(8 * hi + 8, 8), :] = zero

    acc[...] = jnp.zeros_like(acc)

    @pl.when(down_ok)
    def _():
        st_above().wait_recv()

    @pl.when(up_ok)
    def _():
        st_below().wait_recv()

    lane = lax.broadcasted_iota(jnp.int32, (8, 128), 1)

    def lon_diff(xs, c):
        after, before = xs[(c + 1) % wins], xs[c - 1]
        east_of = pltpu.roll(jnp.where(lane == 0, after, xs[c]), 127, 1)
        return east_of - pltpu.roll(jnp.where(lane == 127, before, xs[c]), 1, 1)

    def lat_diff(ref, c, r0):
        return ref[c, pl.ds(r0 + 9, 8), :] - ref[c, pl.ds(r0 + 7, 8), :]

    def run(kind, source, s, lo, hi, finish, target_of=None):
        def push(h, c, at, step):
            if kind != "forced":
                return 0.5 * h
            base = 2 * (s * STEPS + step)
            return 0.5 * (h + (trig[base] * st[2, c, at, :] + trig[base + 1] * st[3, c, at, :]))

        def begin(r, _):
            r0 = pl.multiple_of(8 * r, 8)
            at = pl.ds(r0, 8)
            for c in range(wins):
                raised[c, pl.ds(pl.multiple_of(r0 + 8, 8), 8), :] = push(
                    source[s, c, 0, at, :], c, at, 0
                )
            return 0

        lax.fori_loop(lo, hi, begin, 0)
        edge(lo, hi)
        for step in range(STEPS):
            def first(r, _):
                r0 = pl.multiple_of(8 * r, 8)
                at = pl.ds(r0, 8)
                padded = pl.ds(pl.multiple_of(r0 + 8, 8), 8)
                cor = rows_in[0, at, :]
                xs = [raised[c, padded, :] for c in range(wins)]
                out = []
                for c in range(wins):
                    wet, sea = st[0, c, at, :], st[1, c, at, :]
                    dx, dy = lon_diff(xs, c), lat_diff(raised, c, r0)
                    if step == 0:
                        u, v = source[s, c, 1, at, :], source[s, c, 2, at, :]
                    else:
                        u, v = east[c, at, :], north[c, at, :]
                    if kind == "back":
                        e = sea * (u + wet * dx)
                        f = sea * (v + wet * dy)
                        out.append((
                            DRAG_RATE * e - cor * f, cor * e + DRAG_RATE * f, 0.5 * e, 0.5 * f
                        ))
                    else:
                        e = sea * (DRAG_RATE * u + cor * v - dx)
                        f = sea * (DRAG_RATE * v - cor * u - dy)
                        half = 0.5 * wet
                        out.append((e, f, half * e, half * f))
                for c in range(wins):
                    east[c, at, :], north[c, at, :] = out[c][0], out[c][1]
                    fluy[c, at, :], flux[c, padded, :] = out[c][2], out[c][3]
                return 0

            lax.fori_loop(lo, hi, first, 0)

            def second(r, _):
                r0 = pl.multiple_of(8 * r, 8)
                at = pl.ds(r0, 8)
                inside = rows_in[1, at, :]
                xs = [fluy[c, at, :] for c in range(wins)]
                out = []
                for c in range(wins):
                    d = lon_diff(xs, c) + lat_diff(flux, c, r0)
                    h = source[s, c, 0, at, :] if step == 0 else high[c, at, :]
                    h = (h + d if kind == "back" else h - d) * inside
                    if step == STEPS - 1:
                        out.append(finish(c, at, (h, east[c, at, :], north[c, at, :])))
                    else:
                        out.append((h, push(h, c, at, step + 1)))
                if step < STEPS - 1:
                    ahead = pl.ds(pl.multiple_of(r0 + 8, 8), 8)
                    for c in range(wins):
                        high[c, at, :], raised[c, ahead, :] = out[c]
                elif kind == "free":
                    acc[0] += sum(x for x, _ in out[:-1])
                    acc[1] += sum(x for _, x in out[:-1])
                else:
                    target, slot = target_of
                    for c in range(wins):
                        for a in range(3):
                            target[slot, c, a, at, :] = out[c][a]
                return 0

            inner = 1 if step == STEPS - 1 else 0
            lax.fori_loop(lo + inner, hi - inner, second, 0)

    recv_halo(me)

    def keep(c, at, values):
        return values

    run("forced", start, me, 0, strips, keep, (mis, me))

    for n in range(1, sections - 1):
        piece(turn(n), me).wait_send()
    piece(turn(sections - 1), me).start()

    def arrive(n):
        s = turn(n)
        piece(s, s).wait_recv()
        send_halo(s)

    for n in range(1, sections - 1):
        arrive(n)

    def forced(n, _):
        @pl.when(n == sections - 2)
        def _():
            arrive(sections - 1)

        s = turn(n)
        recv_halo(s)
        run("forced", start, s, 0, strips, keep, (mis, s))
        return 0

    lax.fori_loop(1, sections, forced, 0)

    def subtract(s, after):
        def body(r, _):
            at = pl.ds(pl.multiple_of(8 * r, 8), 8)
            out = [
                [mis[s, c, a, at, :] - start[after, c, a, at, :] for a in range(3)]
                for c in range(wins)
            ]
            for c in range(wins):
                for a in range(3):
                    mis[s, c, a, at, :] = out[c][a]
            return 0

        lax.fori_loop(1, strips - 1, body, 0)

    subtract(me, peer(1))
    columns = pl.ds(me * per, per)
    own_mis = pltpu.make_async_copy(
        mis.at[me, pl.ds(0, per), :, pl.ds(top, rows), :],
        home.at[columns],
        own_sem.at[1],
    )
    own_mis.start()

    def give(source, target, send, recv, s, at_columns, slot):
        return pltpu.make_async_remote_copy(
            src_ref=source.at[s, pl.ds(0, per), :, pl.ds(top, rows), :],
            dst_ref=target.at[at_columns],
            send_sem=send.at[s], recv_sem=recv.at[slot],
            device_id={"sec": s}, device_id_type=MESH,
        )

    def differ(i, _):
        s = peer(i)
        subtract(s, peer(i + 1))
        give(mis, home, s2, r2, s, columns, me).start()
        return 0

    lax.fori_loop(1, sections, differ, 0)

    def back(i, _):
        s = peer(i)
        before = peer(i + sections - 1)

        def done(c, at, values):
            return [x - mis[before, c, a, at, :] for a, x in enumerate(values)]

        run("back", mis, s, 1, strips - 1, done, (grad, s))

        @pl.when(i < sections)
        def _():
            give(grad, full, s3, r3, s, columns, me).start()

        return 0

    lax.fori_loop(1, sections + 1, back, 0)
    own_grad = pltpu.make_async_copy(
        grad.at[me, pl.ds(0, per), :, pl.ds(top, rows), :],
        full.at[columns],
        own_sem.at[2],
    )
    own_grad.start()

    def image(i, _):
        s = peer(i)
        after = peer(i + 1)

        def squares(c, at, values):
            pairs = [(x, grad[after, c, a, at, :]) for a, x in enumerate(values)]
            return sum(g * g for _, g in pairs), sum((x - g) * (x - g) for x, g in pairs)

        run("free", grad, s, 2, strips - 2, squares)
        return 0

    lax.fori_loop(0, sections, image, 0)

    part[me] = acc[...]

    def share_part(j, slot):
        return pltpu.make_async_remote_copy(
            src_ref=acc, dst_ref=part.at[slot], send_sem=ps.at[j], recv_sem=pr.at[slot],
            device_id={"sec": j}, device_id_type=MESH,
        )

    for i in range(1, sections):
        share_part(peer(i), me).start()
    for i in range(1, sections):
        share_part(peer(i), peer(i)).wait_recv()
    for i in range(1, sections):
        share_part(peer(i), me).wait_send()
    summed = part[0]
    for s in range(1, sections):
        summed = summed + part[s]
    acc[...] = summed
    total[band] = summed

    def share_total(j, slot):
        return pltpu.make_async_remote_copy(
            src_ref=acc, dst_ref=total.at[slot], send_sem=ts.at[j], recv_sem=tr.at[slot],
            device_id={"lat": j}, device_id_type=MESH,
        )

    for i in range(1, bands):
        share_total(lax.rem(band + i, bands), band).start()
    for i in range(1, bands):
        j = lax.rem(band + i, bands)
        share_total(j, j).wait_recv()
    summed = total[0]
    for s in range(1, bands):
        summed = summed + total[s]
    sums = jnp.sum(jnp.sum(summed, axis=2, keepdims=True), axis=1, keepdims=True)
    step = sums[0] / count / (sums[1] / count + EPSILON)
    step_out[...] = jnp.broadcast_to(step, (8, 128))

    own_mis.wait()

    def mismatches(i, _):
        s = peer(i)
        give(mis, home, s2, r2, s, columns, s).wait()
        return 0

    lax.fori_loop(1, sections, mismatches, 0)

    own_grad.wait()

    def grads(i, _):
        s = peer(i)
        give(grad, full, s3, r3, s, columns, s).wait_recv()
        return 0

    lax.fori_loop(1, sections, grads, 0)


    piece(turn(sections - 1), me).wait_send()

    def drain(i, _):
        s = peer(i)
        give(grad, full, s3, r3, s, columns, me).wait_send()
        return 0

    lax.fori_loop(1, sections, drain, 0)

    def drain_halo(i, _):
        s = peer(i)

        @pl.when(up_ok)
        def _():
            to_above(s).wait_send()

        @pl.when(down_ok)
        def _():
            to_below(s).wait_send()

        return 0

    lax.fori_loop(0, sections, drain_halo, 0)

    @pl.when(up_ok)
    def _():
        st_above().wait_send()

    @pl.when(down_ok)
    def _():
        st_below().wait_send()

    for i in range(1, bands):
        share_total(lax.rem(band + i, bands), band).wait_send()


def finish_kernel(fields, home, full, step, new_fields, mismatch):
    rows, share = fields.shape[1:]
    length = step[0:1, :]

    def body(r, _):
        at = pl.ds(pl.multiple_of(8 * r, 8), 8)
        for c in range(share // 128):
            cols = slice(c * 128, c * 128 + 128)
            for a in range(3):
                new_fields[a, at, cols] = fields[a, at, cols] - length * full[c, a, at, :]
                mismatch[a, at, cols] = home[c, a, at, :]
        return 0

    lax.fori_loop(0, rows // 8, body, 0)


def shards(states, depth_field, land_mask, tide_cos, tide_sin):
    fields = states[0]
    rows, lon = fields.shape[1:]
    sections, bands = lax.axis_size("sec"), lax.axis_size("lat")
    band = lax.axis_index("lat")
    share = lon // sections
    tall = rows + 2 * HALO
    lat_total = rows * bands
    ids = band * rows - HALO + jnp.arange(tall, dtype=jnp.int32)
    inside = ((ids >= 0) & (ids < lat_total)).astype(jnp.float32)
    coriolis = CORIOLIS_MAX * jnp.sin(
        jnp.pi * (ids.astype(jnp.float32) + 0.5) / lat_total - 0.5 * jnp.pi
    )
    rows_in = jnp.broadcast_to(jnp.stack([coriolis, inside])[:, :, None], (2, tall, 128))
    angles = np.float32(TWO_PI) * np.arange(sections * STEPS, dtype=np.float32) / np.float32(
        sections * STEPS
    )
    trig = jnp.asarray(np.stack([np.cos(angles), np.sin(angles)], axis=1).reshape(-1))
    f32 = jnp.float32
    dma = pltpu.SemaphoreType.DMA
    any_spec = pl.BlockSpec(memory_space=pl.ANY)
    vmem = pl.BlockSpec(memory_space=pltpu.VMEM)
    tiles, wins = lon // 128, share // 128 + 1
    stacked = pltpu.VMEM((sections, wins, 3, tall, 128), f32)
    plain = pltpu.VMEM((wins, tall, 128), f32)
    padded = pltpu.VMEM((wins, tall + 16, 128), f32)
    gathered = jax.ShapeDtypeStruct((tiles, 3, rows, 128), f32)
    home, full, step = pl.pallas_call(
        functools.partial(kernel, sections, bands, float(sections * 3 * lat_total * lon)),
        out_shape=(
            gathered,
            gathered,
            jax.ShapeDtypeStruct((8, 128), f32),
        ),
        in_specs=[any_spec] * 5 + [vmem, pl.BlockSpec(memory_space=pltpu.SMEM)],
        out_specs=(any_spec, any_spec, vmem),
        scratch_shapes=[
            pltpu.VMEM((tiles + sections, 3, rows, 128), f32),
            pltpu.VMEM((wins + 1, rows, 128), jnp.int32),
            pltpu.VMEM((4, wins + 1, tall, 128), f32),
            stacked, stacked, stacked,
            plain, plain, plain, padded, padded, plain,
            pltpu.VMEM((2, 8, 128), f32),
            pltpu.VMEM((sections, 2, 8, 128), f32),
            pltpu.VMEM((bands, 2, 8, 128), f32),
            dma((5,)),
            dma((sections,)), dma((sections,)),
            dma((2, sections)), dma((2, sections)),
            dma((2,)), dma((2,)),
            dma((sections,)), dma((sections,)),
            dma((sections,)), dma((sections,)),
            dma((3,)),
            dma((sections,)), dma((sections,)),
            dma((bands,)), dma((bands,)),
        ],
        compiler_params=pltpu.CompilerParams(
            collective_id=0, has_side_effects=True, vmem_limit_bytes=60 * 1024 * 1024
        ),
        name="shooting",
    )(fields, depth_field, land_mask, tide_cos, tide_sin, rows_in, trig)
    block = pl.BlockSpec((3, rows, share), lambda i: (0, 0, i))
    by_tile = pl.BlockSpec((share // 128, 3, rows, 128), lambda i: (i, 0, 0, 0))
    new_fields, mismatch = pl.pallas_call(
        finish_kernel,
        grid=(sections,),
        out_shape=(jax.ShapeDtypeStruct(fields.shape, f32),) * 2,
        in_specs=[block, by_tile, by_tile, pl.BlockSpec((8, 128), lambda i: (0, 0))],
        out_specs=(block, block),
        compiler_params=pltpu.CompilerParams(vmem_limit_bytes=32 * 1024 * 1024),
        name="update",
    )(fields, home, full, step)
    return new_fields[None], mismatch[None], step[0, 0]


def solution(mesh):
    return jax.shard_map(
        shards,
        mesh=mesh,
        in_specs=(
            P("sec", None, "lat", None),
            P("lat", None),
            P("lat", None),
            P("lat", None),
            P("lat", None),
        ),
        out_specs=(P("sec", None, "lat", None), P("sec", None, "lat", None), P()),
        check_vma=False,
    )
```
